256 devices in a mesh: gx: 16 (over z, y_lo), gy: 8 (over x, y_hi), gz: 2 (over core).
Axes of the slice: x: 4, y: 4 (y_hi: 2, y_lo: 2; y = y_hi * 2 + y_lo), z: 8, core: 2. Of those that a mesh axis runs over, the one named last changes fastest.
Arguments:
- toroidal: float32 [2, 2, 2048, 2048], P(None, 'gz', 'gx', 'gy'), may hold values from -6 to 6
- poloidal: float32 [2, 2, 2048, 2048], P(None, 'gz', 'gx', 'gy'), may hold values from -6 to 6
Outputs:
- velocity: float32 [3, 2, 2, 2048, 2048], P(None, None, 'gz', 'gx', 'gy')
The draws below stay inside these ranges and needn't reach their ends.
All inputs are finite; a program needn't handle non-finite values.
Results may differ from the reference program's by a relative error of at most 0.0001.
Values sent between devices are 32-bit elements; how exact they have to be, the bound alone decides.
No kernel may reach another device: no remote copies, remote signals or barrier semaphores. Data moves between devices by JAX's collectives and lax.ppermute only.
A program may use at most 64 MiB of HBM per device.

```python
import jax
import jax.numpy as jnp

NX = 2048
NY = 2048
KZ = 2
KZ_FIRST = 128
K0 = 512
N_GX = 16


def level_of(own_key, extent, pieces, low, top_value):
    gain = 1.0
    for position, parts in pieces:
        draws = jax.random.uniform(jax.random.fold_in(jax.random.fold_in(own_key, 6), position), (parts,), jnp.float32, low / len(pieces), top_value / len(pieces))
        gain = gain * jnp.repeat(jnp.exp(draws), extent[position] // parts).reshape((-1,) + (1,) * (len(extent) - 1 - position))
    return gain


def normal_values(key, shape, scale, most, cuts=(), kind=jnp.bfloat16):
    factor_of = level_of(key, shape, cuts, -0.22, 0.18) if cuts else 1.0
    array = jax.random.normal(key, shape, jnp.float32) * scale * factor_of
    return jnp.minimum(jnp.maximum(array, -most), most).astype(kind)


def setup_inputs(seed: int = 0) -> dict:
    arg_keys = jax.random.split(jax.random.key(seed), 3)
    toroidal = normal_values(arg_keys[0], (2, KZ, NX, NY), 1.0, 6.0, ((1, 2), (2, 16), (3, 8)), jnp.float32)
    poloidal = normal_values(arg_keys[1], (2, KZ, NX, NY), 1.0, 6.0, ((1, 2), (2, 16), (3, 8)), jnp.float32)
    return dict(toroidal=toroidal, poloidal=poloidal)


def velocity_spectrum(toroidal, poloidal, wave_x, wave_y, wave_z):
    horiz = wave_x * wave_x + wave_y * wave_y
    square = horiz + wave_z * wave_z
    magnitude = jnp.sqrt(square)
    ratio = square / (K0 * K0)
    shaping = 4.0 / NX * ratio * jnp.exp(1.0 - ratio)
    tor_gain = shaping / magnitude
    pol_gain = shaping / square
    tor_re, tor_im = (toroidal[0], toroidal[1])
    pol_re, pol_im = (poloidal[0], poloidal[1])
    cross = wave_z * pol_gain
    first_re = -wave_y * tor_gain * tor_im - wave_x * cross * pol_re
    first_im = wave_y * tor_gain * tor_re - wave_x * cross * pol_im
    second_re = wave_x * tor_gain * tor_im - wave_y * cross * pol_re
    second_im = -wave_x * tor_gain * tor_re - wave_y * cross * pol_im
    third_re = horiz * pol_gain * pol_re
    third_im = horiz * pol_gain * pol_im
    return jnp.stack([jnp.stack([first_re, first_im]), jnp.stack([second_re, second_im]), jnp.stack([third_re, third_im])])

def reverse_bits(values, nbits):
    result = jnp.zeros_like(values)
    for place in range(nbits):
        result = result + jnp.left_shift(jnp.bitwise_and(jnp.right_shift(values, place), 1), nbits - 1 - place)
    return result

def frequencies(total):
    index = jnp.arange(total, dtype=jnp.int32)
    return jnp.where(index < total // 2, index, index - total).astype(jnp.float32)

def reference(toroidal, poloidal):
    wave_x = frequencies(NX)[:, None]
    wave_y = frequencies(NY)[None, :]
    rows = NX // N_GX
    nbits = N_GX.bit_length() - 1
    order = reverse_bits(jnp.arange(N_GX, dtype=jnp.int32), nbits)
    planes = []
    for plane in range(KZ):
        wave_z = jnp.float32(KZ_FIRST + plane)
        spectrum = velocity_spectrum(toroidal[:, plane], poloidal[:, plane], wave_x, wave_y, wave_z)
        components = []
        for comp in range(3):
            values = jnp.fft.ifft2(spectrum[comp, 0] + 1j * spectrum[comp, 1]) * (NX * NY)
            values = values.reshape(rows, N_GX, NY).transpose(1, 0, 2)[order].reshape(NX, NY)
            components.append(jnp.stack([jnp.real(values), jnp.imag(values)]).astype(jnp.float32))
        planes.append(jnp.stack(components))
    return jnp.stack(planes, axis=2)
```

```python
import math

import jax
import jax.numpy as jnp
import numpy as np
from jax import lax
from jax.experimental import pallas as pl
from jax.experimental.pallas import tpu as pltpu
from jax.sharding import PartitionSpec as P

N = 2048
KZ_FIRST = 128
K0 = 512
GX = 16
GY = 8
ROWS = N // GX
COLS = N // GY
LANES = 128
PLANE = ("gx", "gy")


def reversed_bits(value, nbits):
    return sum(((value >> place) & 1) << (nbits - 1 - place) for place in range(nbits))


def outer_table():
    y0 = np.arange(16)[:, None, None, None, None]
    residue = np.array([reversed_bits(d, 4) for d in range(16)])[None, :, None, None, None]
    half = np.arange(2)[None, None, :, None, None]
    high = np.arange(16)[None, None, None, :, None]
    block = np.arange(8)[None, None, None, None, :]
    phase = (high * residue + (2 * block + half) * y0) % 16
    angle = (2.0 * math.pi / 16) * phase.reshape(256, 256)
    cos, sin = np.cos(angle), np.sin(angle)
    return np.block([[cos, -sin], [sin, cos]]).astype(np.float32)


def lane_table():
    lane = np.arange(LANES)
    y1 = 16 * (lane & 7) + 8 * ((lane >> 3) & 1) + (lane >> 4)
    angle = (2.0 * math.pi / LANES) * (lane[:, None] * y1[None, :] % LANES)
    cos, sin = np.cos(angle), np.sin(angle)
    return np.block([[cos, sin], [-sin, cos]]).astype(np.float32)


def twist_table():
    angle = (2.0 * math.pi / N) * (np.arange(16)[:, None] * np.arange(LANES)[None, :] % N)
    return np.stack([np.cos(angle), np.sin(angle)]).astype(np.float32)


def row_table():
    index = np.arange(ROWS)
    angle = (2.0 * math.pi / ROWS) * (index[:, None] * index[None, :] % ROWS)
    cos, sin = np.cos(angle), np.sin(angle)
    return np.block([[cos, -sin], [sin, cos]]).astype(np.float32)


def halves(value):
    high = value.astype(jnp.bfloat16)
    return high, (value - high.astype(jnp.float32)).astype(jnp.bfloat16)


def mac(left_high, left_low, right_high, right_low):
    def dot(left, right):
        return jnp.dot(left, right, preferred_element_type=jnp.float32)

    return dot(left_high, right_high) + (dot(left_high, right_low) + dot(left_low, right_high))


def pack_kernel(tor_ref, pol_ref, out_ref):
    for part in range(4):
        source = tor_ref if part < 2 else pol_ref
        for half in range(2):
            out_ref[pl.ds(part * 2 + half, ROWS, stride=8), :] = source[
                part % 2, 0, :, half * LANES : (half + 1) * LANES
            ]


def plane_kernel(in_ref, outer_ref, lane_ref, twist_ref, out_ref, high_ref, low_ref):
    low_x = lax.axis_index("gx") * GY + lax.axis_index("gy")
    wave_z = (KZ_FIRST + lax.axis_index("gz")).astype(jnp.float32)
    row = lax.broadcasted_iota(jnp.int32, (ROWS, LANES), 0)
    lane = lax.broadcasted_iota(jnp.int32, (ROWS, LANES), 1)
    glob_x = (row >> 3) * ROWS + low_x
    wave_x = jnp.where(glob_x < N // 2, glob_x, glob_x - N).astype(jnp.float32)
    for half in range(2):
        glob_y = (row & 7) * COLS + (half * LANES + lane)
        wave_y = jnp.where(glob_y < N // 2, glob_y, glob_y - N).astype(jnp.float32)
        horiz = wave_x * wave_x + wave_y * wave_y
        square = horiz + wave_z * wave_z
        pol_gain = (4.0 / N / (K0 * K0)) * jnp.exp(1.0 - square * (1.0 / (K0 * K0)))
        tor_gain = pol_gain * jnp.sqrt(square)
        parts = [in_ref[pl.ds(part * 2 + half, ROWS, stride=8), :] for part in range(4)]
        tor_re, tor_im = parts[0] * tor_gain, parts[1] * tor_gain
        pol_re, pol_im = parts[2] * pol_gain, parts[3] * pol_gain
        cross_x, cross_y = wave_x * wave_z, wave_y * wave_z
        spectrum = [
            (-wave_y * tor_im - cross_x * pol_re, wave_y * tor_re - cross_x * pol_im),
            (wave_x * tor_im - cross_y * pol_re, -wave_x * tor_re - cross_y * pol_im),
            (horiz * pol_re, horiz * pol_im),
        ]
        for comp in range(3):
            for imag in range(2):
                high, low = halves(spectrum[comp][imag])
                at = pl.ds(imag * 256 + half * ROWS, ROWS), pl.ds(comp * LANES, LANES)
                high_ref[at] = high
                low_ref[at] = low
    residue = reversed_bits(lax.broadcasted_iota(jnp.int32, (GX, LANES), 0), 4)
    angle = (low_x * residue % N).astype(jnp.float32) * (2.0 * math.pi / N)
    turn_re, turn_im = jnp.cos(angle)[None], jnp.sin(angle)[None]
    beta_re, beta_im = twist_ref[0][:, None, :], twist_ref[1][:, None, :]
    twist_re = (beta_re * turn_re - beta_im * turn_im).reshape(256, LANES)
    twist_im = (beta_re * turn_im + beta_im * turn_re).reshape(256, LANES)
    outer_high, outer_low = halves(outer_ref[...])
    lane_high, lane_low = halves(lane_ref[...])
    lane_bit = lax.broadcasted_iota(jnp.int32, (GX, LANES), 1)
    for comp in range(3):
        cols = slice(comp * LANES, (comp + 1) * LANES)
        value = mac(outer_high, outer_low, high_ref[:, cols], low_ref[:, cols])
        real, imag = value[:256], value[256:]
        turned = jnp.concatenate(
            [real * twist_re - imag * twist_im, real * twist_im + imag * twist_re], axis=1
        )
        high, low = halves(turned)
        value = mac(high, low, lane_high, lane_low)
        for imag in range(2):
            tiles = [
                value[y0 * GX : (y0 + 1) * GX, imag * LANES : (imag + 1) * LANES] for y0 in range(16)
            ]
            for place in range(4):
                step = 1 << place
                upper = (lane_bit & step) != 0
                swapped = list(tiles)
                for index in range(16):
                    if index & step:
                        continue
                    first, second = tiles[index], tiles[index | step]
                    swapped[index] = jnp.where(upper, pltpu.roll(second, step, 1), first)
                    swapped[index | step] = jnp.where(
                        upper, second, pltpu.roll(first, LANES - step, 1)
                    )
                tiles = swapped
            for index in range(16):
                start = (index & 7) * 12 + (comp * 2 + imag) * 2 + (index >> 3)
                out_ref[pl.ds(start, GX, stride=96), :] = tiles[index]


def row_kernel(in_ref, table_ref, out_ref):
    table_high, table_low = halves(table_ref[...])
    for comp in range(3):
        parts = [
            jnp.concatenate(
                [in_ref[pl.ds((comp * 2 + imag) * 2 + half, ROWS, stride=12), :] for half in range(2)],
                axis=1,
            )
            for imag in range(2)
        ]
        high, low = halves(jnp.concatenate(parts, axis=0))
        value = mac(table_high, table_low, high, low)
        out_ref[comp, 0, 0] = value[:ROWS]
        out_ref[comp, 1, 0] = value[ROWS:]


def exchange(value):
    chunks = value.reshape(GX * GY, 1, -1)
    return lax.all_to_all(chunks, PLANE, 0, 0, tiled=True).reshape(-1, LANES)


def local(toroidal, poloidal):
    vmem = pl.BlockSpec(memory_space=pltpu.VMEM)
    packed = pl.pallas_call(
        pack_kernel,
        out_shape=jax.ShapeDtypeStruct((ROWS * 8, LANES), jnp.float32),
        in_specs=[vmem, vmem],
        out_specs=vmem,
    )(toroidal, poloidal)
    spread = exchange(packed)
    lines = pl.pallas_call(
        plane_kernel,
        out_shape=jax.ShapeDtypeStruct((ROWS * 12, LANES), jnp.float32),
        in_specs=[vmem] * 4,
        out_specs=vmem,
        scratch_shapes=[pltpu.VMEM((512, 3 * LANES), jnp.bfloat16)] * 2,
        compiler_params=pltpu.CompilerParams(vmem_limit_bytes=32 * 2**20),
    )(spread, outer_table(), lane_table(), twist_table())
    gathered = exchange(lines)
    return pl.pallas_call(
        row_kernel,
        out_shape=jax.ShapeDtypeStruct((3, 2, 1, ROWS, COLS), jnp.float32),
        in_specs=[vmem, vmem],
        out_specs=vmem,
        compiler_params=pltpu.CompilerParams(vmem_limit_bytes=32 * 2**20),
    )(gathered, row_table())


def solution(mesh):
    in_specs = (P(None, "gz", "gx", "gy"), P(None, "gz", "gx", "gy"))
    out_specs = P(None, None, "gz", "gx", "gy")
    return jax.shard_map(local, mesh=mesh, in_specs=in_specs, out_specs=out_specs, check_vma=False)
```

```python
import math

import jax
import jax.numpy as jnp
import ml_dtypes
import numpy as np
from jax import lax
from jax.experimental import pallas as pl
from jax.experimental.pallas import tpu as pltpu
from jax.sharding import PartitionSpec as P

N = 2048
KZ_FIRST = 128
K0 = 512
GX = 16
GY = 8
ROWS = N // GX
COLS = N // GY
LANES = 128
PLANE = ("gx", "gy")


def reversed_bits(value, nbits):
    return sum(((value >> place) & 1) << (nbits - 1 - place) for place in range(nbits))


def split_table(values, axis):
    high = values.astype(ml_dtypes.bfloat16)
    low = (values - high.astype(np.float64)).astype(ml_dtypes.bfloat16)
    return np.concatenate([high, low], axis)


def outer_tables():
    y0 = np.arange(8)[:, None, None, None]
    residue = np.array([reversed_bits(d, 4) for d in range(GX)])[None, :, None, None]
    high = np.arange(GX)[None, None, :, None]
    block = np.arange(GY)[None, None, None, :]
    tables = []
    for half in range(2):
        phase = (high * residue + (2 * block + half) * y0) % 16
        angle = (2.0 * math.pi / 16) * phase.reshape(128, 128)
        cos, sin = np.cos(angle), np.sin(angle)
        tables.append(split_table(np.block([[cos, -sin], [sin, cos]]), 1))
    return np.stack(tables)


def lane_table():
    lane = np.arange(LANES)
    y1 = 16 * (lane & 7) + 8 * ((lane >> 3) & 1) + (lane >> 4)
    angle = (2.0 * math.pi / LANES) * (lane[:, None] * y1[None, :] % LANES)
    cos, sin = np.cos(angle), np.sin(angle)
    return split_table(np.block([[cos, sin], [-sin, cos]]), 0)


def twist_table():
    angle = (2.0 * math.pi / N) * (np.arange(16)[:, None] * np.arange(LANES)[None, :] % N)
    return np.stack([np.cos(angle), np.sin(angle)]).astype(np.float32)


def row_table():
    index = np.arange(ROWS)
    angle = (2.0 * math.pi / ROWS) * (index[:, None] * index[None, :] % ROWS)
    cos, sin = np.cos(angle), np.sin(angle)
    return split_table(np.block([[cos, -sin], [sin, cos]]), 1)


def halves(value):
    high = value.astype(jnp.bfloat16)
    return high, (value - high.astype(jnp.float32)).astype(jnp.bfloat16)


def dot(left, right):
    return jnp.dot(left, right, preferred_element_type=jnp.float32)


def table_times(table, high, low):
    wide = jnp.concatenate([table, table[:, : table.shape[1] // 2]], axis=1)
    return dot(wide, jnp.concatenate([high, high, low], axis=0))


def pack_kernel(tor_ref, pol_ref, out_ref):
    for part in range(4):
        source = tor_ref if part < 2 else pol_ref
        for half in range(2):
            out_ref[pl.ds(part * 2 + half, ROWS, stride=8), :] = source[
                part % 2, 0, :, half * LANES : (half + 1) * LANES
            ]


def plane_kernel(in_ref, outer_ref, lane_ref, twist_ref, out_ref, high_ref, low_ref):
    low_x = lax.axis_index("gx") * GY + lax.axis_index("gy")
    wave_z = (KZ_FIRST + lax.axis_index("gz")).astype(jnp.float32)
    row = lax.broadcasted_iota(jnp.int32, (ROWS, LANES), 0)
    lane = lax.broadcasted_iota(jnp.int32, (ROWS, LANES), 1)
    glob_x = (row >> 3) * ROWS + low_x
    wave_x = jnp.where(glob_x < N // 2, glob_x, glob_x - N).astype(jnp.float32)
    for half in range(2):
        glob_y = (row & 7) * COLS + (half * LANES + lane)
        wave_y = jnp.where(glob_y < N // 2, glob_y, glob_y - N).astype(jnp.float32)
        horiz = wave_x * wave_x + wave_y * wave_y
        square = horiz + wave_z * wave_z
        pol_gain = (4.0 / N / (K0 * K0)) * jnp.exp(1.0 - square * (1.0 / (K0 * K0)))
        tor_gain = pol_gain * jnp.sqrt(square)
        parts = [in_ref[pl.ds(part * 2 + half, ROWS, stride=8), :] for part in range(4)]
        tor_re, tor_im = parts[0] * tor_gain, parts[1] * tor_gain
        pol_re, pol_im = parts[2] * pol_gain, parts[3] * pol_gain
        cross_x, cross_y = wave_x * wave_z, wave_y * wave_z
        spectrum = [
            (-wave_y * tor_im - cross_x * pol_re, wave_y * tor_re - cross_x * pol_im),
            (wave_x * tor_im - cross_y * pol_re, -wave_x * tor_re - cross_y * pol_im),
            (horiz * pol_re, horiz * pol_im),
        ]
        for comp in range(3):
            for imag in range(2):
                high, low = halves(spectrum[comp][imag])
                at = half, pl.ds(imag * ROWS, ROWS), pl.ds(comp * LANES, LANES)
                high_ref[at] = high
                low_ref[at] = low
    residue = reversed_bits(lax.broadcasted_iota(jnp.int32, (GX, LANES), 0), 4)
    angle = (low_x * residue % N).astype(jnp.float32) * (2.0 * math.pi / N)
    turn_re, turn_im = jnp.cos(angle)[None], jnp.sin(angle)[None]
    beta_re, beta_im = twist_ref[0][:, None, :], twist_ref[1][:, None, :]
    twist_re = (beta_re * turn_re - beta_im * turn_im).reshape(256, LANES)
    twist_im = (beta_re * turn_im + beta_im * turn_re).reshape(256, LANES)
    table = lane_ref[...]
    lane_wide = jnp.concatenate([table[:256], table[:256], table[256:]], axis=0)
    lane_bit = lax.broadcasted_iota(jnp.int32, (GX, LANES), 1)
    even, odd = [table_times(outer_ref[h], high_ref[h], low_ref[h]) for h in range(2)]
    for comp in range(3):
        cols = slice(comp * LANES, (comp + 1) * LANES)
        total, differ = even[:, cols] + odd[:, cols], even[:, cols] - odd[:, cols]
        real = jnp.concatenate([total[:ROWS], differ[:ROWS]], axis=0)
        imag = jnp.concatenate([total[ROWS:], differ[ROWS:]], axis=0)
        turned = jnp.concatenate(
            [real * twist_re - imag * twist_im, real * twist_im + imag * twist_re], axis=1
        )
        high, low = halves(turned)
        value = dot(jnp.concatenate([high, low, high], axis=1), lane_wide)
        for imag in range(2):
            tiles = [
                value[y0 * GX : (y0 + 1) * GX, imag * LANES : (imag + 1) * LANES] for y0 in range(16)
            ]
            for place in range(4):
                step = 1 << place
                upper = (lane_bit & step) != 0
                swapped = list(tiles)
                for index in range(16):
                    if index & step:
                        continue
                    first, second = tiles[index], tiles[index | step]
                    swapped[index] = jnp.where(upper, pltpu.roll(second, step, 1), first)
                    swapped[index | step] = jnp.where(
                        upper, second, pltpu.roll(first, LANES - step, 1)
                    )
                tiles = swapped
            for index in range(16):
                start = (index & 7) * 12 + (comp * 2 + imag) * 2 + (index >> 3)
                out_ref[pl.ds(start, GX, stride=96), :] = tiles[index]


def row_kernel(in_ref, table_ref, out_ref):
    for comp in range(3):
        parts = [
            jnp.concatenate(
                [in_ref[pl.ds((comp * 2 + imag) * 2 + half, ROWS, stride=12), :] for half in range(2)],
                axis=1,
            )
            for imag in range(2)
        ]
        high, low = halves(jnp.concatenate(parts, axis=0))
        value = table_times(table_ref[...], high, low)
        out_ref[comp, 0, 0] = value[:ROWS]
        out_ref[comp, 1, 0] = value[ROWS:]


def exchange(value):
    chunks = value.reshape(GX * GY, 1, -1)
    return lax.all_to_all(chunks, PLANE, 0, 0, tiled=True).reshape(-1, LANES)


def local(toroidal, poloidal):
    vmem = pl.BlockSpec(memory_space=pltpu.VMEM)
    packed = pl.pallas_call(
        pack_kernel,
        out_shape=jax.ShapeDtypeStruct((ROWS * 8, LANES), jnp.float32),
        in_specs=[vmem, vmem],
        out_specs=vmem,
    )(toroidal, poloidal)
    spread = exchange(packed)
    lines = pl.pallas_call(
        plane_kernel,
        out_shape=jax.ShapeDtypeStruct((ROWS * 12, LANES), jnp.float32),
        in_specs=[vmem] * 4,
        out_specs=vmem,
        scratch_shapes=[pltpu.VMEM((2, 256, 3 * LANES), jnp.bfloat16)] * 2,
        compiler_params=pltpu.CompilerParams(vmem_limit_bytes=32 * 2**20),
    )(spread, outer_tables(), lane_table(), twist_table())
    gathered = exchange(lines)
    return pl.pallas_call(
        row_kernel,
        out_shape=jax.ShapeDtypeStruct((3, 2, 1, ROWS, COLS), jnp.float32),
        in_specs=[vmem, vmem],
        out_specs=vmem,
        compiler_params=pltpu.CompilerParams(vmem_limit_bytes=32 * 2**20),
    )(gathered, row_table())


def solution(mesh):
    in_specs = (P(None, "gz", "gx", "gy"), P(None, "gz", "gx", "gy"))
    out_specs = P(None, None, "gz", "gx", "gy")
    return jax.shard_map(local, mesh=mesh, in_specs=in_specs, out_specs=out_specs, check_vma=False)
```

```python
import math

import jax
import jax.numpy as jnp
import ml_dtypes
import numpy as np
from jax import lax
from jax.experimental import pallas as pl
from jax.experimental.pallas import tpu as pltpu
from jax.sharding import PartitionSpec as P

N = 2048
KZ_FIRST = 128
K0 = 512
GX = 16
GY = 8
ROWS = N // GX
COLS = N // GY
LANES = 128
PLANE = ("gx", "gy", "gz")
GX_ORDER = [11, 7, 15, 6, 13, 5, 9, 4, 10, 3, 12, 2, 8, 1, 14, 0]
GY_ORDER = [7, 5, 3, 6, 1, 4, 2, 0]
ORDER = [gx * GY + gy for gx in GX_ORDER for gy in GY_ORDER]


def reversed_bits(value, nbits):
    return sum(((value >> place) & 1) << (nbits - 1 - place) for place in range(nbits))


def split_table(values, axis):
    high = values.astype(ml_dtypes.bfloat16)
    low = (values - high.astype(np.float64)).astype(ml_dtypes.bfloat16)
    return np.concatenate([high, low], axis)


def outer_tables():
    y0 = np.arange(8)[:, None, None]
    residue = np.array([reversed_bits(d, 4) for d in GX_ORDER])[None, :, None]
    high = (np.array(ORDER) // GY)[None, None, :]
    block = (np.array(ORDER) % GY)[None, None, :]
    tables = []
    for half in range(2):
        phase = (high * residue + (2 * block + half) * y0) % 16
        angle = (2.0 * math.pi / 16) * phase.reshape(128, 128)
        cos, sin = np.cos(angle), np.sin(angle)
        tables.append(split_table(np.block([[cos, -sin], [sin, cos]]), 1))
    return np.stack(tables)


def lane_table():
    lane = np.arange(LANES)
    y1 = 16 * np.array(GY_ORDER)[lane & 7] + 8 * ((lane >> 3) & 1) + (lane >> 4)
    angle = (2.0 * math.pi / LANES) * (lane[:, None] * y1[None, :] % LANES)
    cos, sin = np.cos(angle), np.sin(angle)
    return split_table(np.block([[cos, sin], [-sin, cos]]), 0)


def twist_table():
    angle = (2.0 * math.pi / N) * (np.arange(16)[:, None] * np.arange(LANES)[None, :] % N)
    return np.stack([np.cos(angle), np.sin(angle)]).astype(np.float32)


def row_table():
    index = np.arange(ROWS)
    angle = (2.0 * math.pi / ROWS) * (index[:, None] * index[None, :] % ROWS)
    cos, sin = np.cos(angle), np.sin(angle)
    return split_table(np.block([[cos, -sin], [sin, cos]]), 1)


def turn_table():
    residue = np.array([reversed_bits(d, 4) for d in GX_ORDER], np.float32) / N
    return np.broadcast_to(residue[:, None], (GX, LANES)).copy()


def wave_table():
    sender = np.array(ORDER)
    base_x = (sender // GY + GX // 2) % GX * ROWS - N // 2
    base_y = (sender % GY + GY // 2) % GY * COLS - N // 2
    rows = np.stack([base_x, base_y]).astype(np.float32)
    return np.broadcast_to(rows[:, :, None], (2, ROWS, LANES)).copy()


def halves(value):
    high = value.astype(jnp.bfloat16)
    return high, (value - high.astype(jnp.float32)).astype(jnp.bfloat16)


def dot(left, right):
    return jnp.dot(left, right, preferred_element_type=jnp.float32)


def table_times(table, high, low):
    wide = jnp.concatenate([table, table[:, : table.shape[1] // 2]], axis=1)
    return dot(wide, jnp.concatenate([high, high, low], axis=0))


def pack_kernel(tor_ref, pol_ref, out_ref):
    for part in range(4):
        source = tor_ref if part < 2 else pol_ref
        for half in range(2):
            out_ref[pl.ds(part * 2 + half, ROWS, stride=8), :] = source[
                part % 2, 0, :, half * LANES : (half + 1) * LANES
            ]


def place_in(order, device):
    return sum(jnp.where(device == entry, place, 0) for place, entry in enumerate(order))


def plane_kernel(
    in_ref, outer_ref, lane_ref, twist_ref, turn_ref, wave_ref, out_ref, high_ref, low_ref
):
    low_x = place_in(GX_ORDER, lax.axis_index("gx")) * GY + place_in(GY_ORDER, lax.axis_index("gy"))
    wave_z = (KZ_FIRST + lax.axis_index("gz")).astype(jnp.float32)
    lane = lax.broadcasted_iota(jnp.int32, (ROWS, LANES), 1).astype(jnp.float32)
    wave_x = wave_ref[0] + low_x.astype(jnp.float32)
    for half in range(2):
        wave_y = wave_ref[1] + (lane + half * LANES)
        horiz = wave_x * wave_x + wave_y * wave_y
        square = horiz + wave_z * wave_z
        pol_gain = (4.0 / N / (K0 * K0)) * jnp.exp(1.0 - square * (1.0 / (K0 * K0)))
        tor_gain = pol_gain * jnp.sqrt(square)
        parts = [in_ref[pl.ds(part * 2 + half, ROWS, stride=8), :] for part in range(4)]
        tor_re, tor_im = parts[0] * tor_gain, parts[1] * tor_gain
        pol_re, pol_im = parts[2] * pol_gain, parts[3] * pol_gain
        cross_x, cross_y = wave_x * wave_z, wave_y * wave_z
        spectrum = [
            (-wave_y * tor_im - cross_x * pol_re, wave_y * tor_re - cross_x * pol_im),
            (wave_x * tor_im - cross_y * pol_re, -wave_x * tor_re - cross_y * pol_im),
            (horiz * pol_re, horiz * pol_im),
        ]
        for comp in range(3):
            for imag in range(2):
                high, low = halves(spectrum[comp][imag])
                at = half, pl.ds(imag * ROWS, ROWS), pl.ds(comp * LANES, LANES)
                high_ref[at] = high
                low_ref[at] = low
    turns = low_x.astype(jnp.float32) * turn_ref[...]
    angle = (turns - jnp.floor(turns)) * (2.0 * math.pi)
    turn_re, turn_im = jnp.cos(angle)[None], jnp.sin(angle)[None]
    beta_re, beta_im = twist_ref[0][:, None, :], twist_ref[1][:, None, :]
    twist_re = (beta_re * turn_re - beta_im * turn_im).reshape(256, LANES)
    twist_im = (beta_re * turn_im + beta_im * turn_re).reshape(256, LANES)
    table = lane_ref[...]
    lane_wide = jnp.concatenate([table[:256], table[:256], table[256:]], axis=0)
    lane_bit = lax.broadcasted_iota(jnp.int32, (GX, LANES), 1)
    even, odd = [table_times(outer_ref[h], high_ref[h], low_ref[h]) for h in range(2)]
    for comp in range(3):
        cols = slice(comp * LANES, (comp + 1) * LANES)
        total, differ = even[:, cols] + odd[:, cols], even[:, cols] - odd[:, cols]
        real = jnp.concatenate([total[:ROWS], differ[:ROWS]], axis=0)
        imag = jnp.concatenate([total[ROWS:], differ[ROWS:]], axis=0)
        turned = jnp.concatenate(
            [real * twist_re - imag * twist_im, real * twist_im + imag * twist_re], axis=1
        )
        high, low = halves(turned)
        value = dot(jnp.concatenate([high, low, high], axis=1), lane_wide)
        for imag in range(2):
            tiles = [
                value[y0 * GX : (y0 + 1) * GX, imag * LANES : (imag + 1) * LANES] for y0 in range(16)
            ]
            for place in range(4):
                step = 1 << place
                upper = (lane_bit & step) != 0
                swapped = list(tiles)
                for index in range(16):
                    if index & step:
                        continue
                    first, second = tiles[index], tiles[index | step]
                    swapped[index] = jnp.where(upper, pltpu.roll(second, step, 1), first)
                    swapped[index | step] = jnp.where(
                        upper, second, pltpu.roll(first, LANES - step, 1)
                    )
                tiles = swapped
            for index in range(16):
                start = (index & 7) * 12 + (comp * 2 + imag) * 2 + (index >> 3)
                out_ref[pl.ds(start, GX, stride=96), :] = tiles[index]


def row_kernel(in_ref, table_ref, out_ref):
    for comp in range(3):
        parts = [
            jnp.concatenate(
                [in_ref[pl.ds((comp * 2 + imag) * 2 + half, ROWS, stride=12), :] for half in range(2)],
                axis=1,
            )
            for imag in range(2)
        ]
        high, low = halves(jnp.concatenate(parts, axis=0))
        value = table_times(table_ref[...], high, low)
        out_ref[comp, 0, 0] = value[:ROWS]
        out_ref[comp, 1, 0] = value[ROWS:]


def exchange(value):
    chunks = value.reshape(GX * GY, 1, -1)
    groups = [[device * 2 + plane for device in ORDER] for plane in range(2)]
    moved = lax.all_to_all(chunks, PLANE, 0, 0, axis_index_groups=groups, tiled=True)
    return moved.reshape(-1, LANES)


def local(toroidal, poloidal):
    vmem = pl.BlockSpec(memory_space=pltpu.VMEM)
    packed = pl.pallas_call(
        pack_kernel,
        out_shape=jax.ShapeDtypeStruct((ROWS * 8, LANES), jnp.float32),
        in_specs=[vmem, vmem],
        out_specs=vmem,
    )(toroidal, poloidal)
    spread = exchange(packed)
    lines = pl.pallas_call(
        plane_kernel,
        out_shape=jax.ShapeDtypeStruct((ROWS * 12, LANES), jnp.float32),
        in_specs=[vmem] * 6,
        out_specs=vmem,
        scratch_shapes=[pltpu.VMEM((2, 256, 3 * LANES), jnp.bfloat16)] * 2,
        compiler_params=pltpu.CompilerParams(vmem_limit_bytes=32 * 2**20),
    )(spread, outer_tables(), lane_table(), twist_table(), turn_table(), wave_table())
    gathered = exchange(lines)
    return pl.pallas_call(
        row_kernel,
        out_shape=jax.ShapeDtypeStruct((3, 2, 1, ROWS, COLS), jnp.float32),
        in_specs=[vmem, vmem],
        out_specs=vmem,
        compiler_params=pltpu.CompilerParams(vmem_limit_bytes=32 * 2**20),
    )(gathered, row_table())


def solution(mesh):
    in_specs = (P(None, "gz", "gx", "gy"), P(None, "gz", "gx", "gy"))
    out_specs = P(None, None, "gz", "gx", "gy")
    return jax.shard_map(local, mesh=mesh, in_specs=in_specs, out_specs=out_specs, check_vma=False)
```

```python
import math

import jax
import jax.numpy as jnp
import ml_dtypes
import numpy as np
from jax import lax
from jax.experimental import pallas as pl
from jax.experimental.pallas import tpu as pltpu
from jax.sharding import PartitionSpec as P

N = 2048
KZ_FIRST = 128
K0 = 512
GX = 16
GY = 8
ROWS = N // GX
COLS = N // GY
LANES = 128
PLANE = ("gx", "gy", "gz")
GX_ORDER = [11, 7, 15, 6, 13, 5, 9, 4, 10, 3, 12, 2, 8, 1, 14, 0]
GY_ORDER = [7, 5, 3, 6, 1, 4, 2, 0]
ORDER = [gx * GY + gy for gx in GX_ORDER for gy in GY_ORDER]


def reversed_bits(value, nbits):
    return sum(((value >> place) & 1) << (nbits - 1 - place) for place in range(nbits))


def split_table(values, axis):
    high = values.astype(ml_dtypes.bfloat16)
    low = (values - high.astype(np.float64)).astype(ml_dtypes.bfloat16)
    return np.concatenate([high, low], axis)


def outer_tables():
    y0 = np.arange(8)[:, None, None]
    residue = np.array([reversed_bits(d, 4) for d in GX_ORDER])[None, :, None]
    high = (np.array(ORDER) // GY)[None, None, :]
    block = (np.array(ORDER) % GY)[None, None, :]
    tables = []
    for half in range(2):
        phase = (high * residue + (2 * block + half) * y0) % 16
        angle = (2.0 * math.pi / 16) * phase.reshape(128, 128)
        cos, sin = np.cos(angle), np.sin(angle)
        tables.append(split_table(np.block([[cos, -sin], [sin, cos]]), 1))
    return np.stack(tables)


def lane_table():
    lane = np.arange(LANES)
    y1 = 8 * (lane & 15) + (lane >> 4)
    angle = (2.0 * math.pi / LANES) * (lane[:, None] * y1[None, :] % LANES)
    cos, sin = np.cos(angle), np.sin(angle)
    return split_table(np.block([[cos, sin], [-sin, cos]]), 0)


def twist_table():
    angle = (2.0 * math.pi / N) * (-127 * np.arange(16)[:, None] * np.arange(LANES)[None, :] % N)
    return np.stack([np.cos(angle), np.sin(angle)]).astype(np.float32)


def row_table():
    index = np.arange(ROWS)
    angle = (2.0 * math.pi / ROWS) * (index[:, None] * index[None, :] % ROWS)
    cos, sin = np.cos(angle), np.sin(angle)
    return split_table(np.block([[cos, -sin], [sin, cos]]), 1)


def turn_table():
    residue = np.array([reversed_bits(d, 4) for d in GX_ORDER], np.float32) / N
    return np.broadcast_to(residue[:, None], (GX, LANES)).copy()


def wave_table():
    sender = np.array(ORDER)
    base_x = (sender // GY + GX // 2) % GX * ROWS - N // 2
    base_y = (sender % GY + GY // 2) % GY * COLS - N // 2
    rows = np.stack([base_x, base_y]).astype(np.float32)
    return np.broadcast_to(rows[:, :, None], (2, ROWS, LANES)).copy()


def halves(value):
    high = value.astype(jnp.bfloat16)
    return high, (value - high.astype(jnp.float32)).astype(jnp.bfloat16)


def dot(left, right):
    return jnp.dot(left, right, preferred_element_type=jnp.float32)


def table_times(table, high, low):
    wide = jnp.concatenate([table, table[:, : table.shape[1] // 2]], axis=1)
    return dot(wide, jnp.concatenate([high, high, low], axis=0))


def place_in(order, device):
    return sum(jnp.where(device == entry, place, 0) for place, entry in enumerate(order))


def plane_kernel(
    in_ref, outer_ref, lane_ref, twist_ref, turn_ref, wave_ref, out_ref, high_ref, low_ref
):
    low_x = place_in(GX_ORDER, lax.axis_index("gx")) * GY + place_in(GY_ORDER, lax.axis_index("gy"))
    wave_z = (KZ_FIRST + lax.axis_index("gz")).astype(jnp.float32)
    lane = lax.broadcasted_iota(jnp.int32, (ROWS, LANES), 1).astype(jnp.float32)
    wave_x = wave_ref[0] + low_x.astype(jnp.float32)
    for half in range(2):
        wave_y = wave_ref[1] + (lane + half * LANES)
        horiz = wave_x * wave_x + wave_y * wave_y
        square = horiz + wave_z * wave_z
        pol_gain = (4.0 / N / (K0 * K0)) * jnp.exp(1.0 - square * (1.0 / (K0 * K0)))
        tor_gain = pol_gain * jnp.sqrt(square)
        parts = [in_ref[pl.ds(part * 2 + half, ROWS, stride=8), :] for part in range(4)]
        tor_re, tor_im = parts[0] * tor_gain, parts[1] * tor_gain
        pol_re, pol_im = parts[2] * pol_gain, parts[3] * pol_gain
        cross_x, cross_y = wave_x * wave_z, wave_y * wave_z
        spectrum = [
            (-wave_y * tor_im - cross_x * pol_re, wave_y * tor_re - cross_x * pol_im),
            (wave_x * tor_im - cross_y * pol_re, -wave_x * tor_re - cross_y * pol_im),
            (horiz * pol_re, horiz * pol_im),
        ]
        for comp in range(3):
            for imag in range(2):
                high, low = halves(spectrum[comp][imag])
                at = half, pl.ds(imag * ROWS, ROWS), pl.ds(comp * LANES, LANES)
                high_ref[at] = high
                low_ref[at] = low
    turns = low_x.astype(jnp.float32) * turn_ref[...]
    angle = (turns - jnp.floor(turns)) * (2.0 * math.pi)
    turn_re, turn_im = jnp.cos(angle)[None], jnp.sin(angle)[None]
    beta_re, beta_im = twist_ref[0][:, None, :], twist_ref[1][:, None, :]
    twist_re = (beta_re * turn_re - beta_im * turn_im).reshape(256, LANES)
    twist_im = (beta_re * turn_im + beta_im * turn_re).reshape(256, LANES)
    table = lane_ref[...]
    lane_wide = jnp.concatenate([table[:256], table[:256], table[256:]], axis=0)
    lane_bit = lax.broadcasted_iota(jnp.int32, (GX, LANES), 1)
    even, odd = [table_times(outer_ref[h], high_ref[h], low_ref[h]) for h in range(2)]
    for comp in range(3):
        cols = slice(comp * LANES, (comp + 1) * LANES)
        total, differ = even[:, cols] + odd[:, cols], even[:, cols] - odd[:, cols]
        real = jnp.concatenate([total[:ROWS], differ[:ROWS]], axis=0)
        imag = jnp.concatenate([total[ROWS:], differ[ROWS:]], axis=0)
        turned = jnp.concatenate(
            [real * twist_re - imag * twist_im, real * twist_im + imag * twist_re], axis=1
        )
        high, low = halves(turned)
        value = dot(jnp.concatenate([high, low, high], axis=1), lane_wide)
        for imag in range(2):
            tiles = [
                value[y0 * GX : (y0 + 1) * GX, imag * LANES : (imag + 1) * LANES] for y0 in range(16)
            ]
            for place in range(4):
                step = 1 << place
                upper = (lane_bit & step) != 0
                tiles = [jnp.where(upper, tiles[(t + step) % 16], tiles[t]) for t in range(16)]
            for index in range(16):
                tile = tiles[-index % 16]
                if index:
                    source = (lane_bit & 112) + ((lane_bit + index) & 15)
                    tile = jnp.take_along_axis(tile, source, axis=1, mode="promise_in_bounds")
                start = GY_ORDER.index(index >> 1) * 12 + (comp * 2 + imag) * 2 + (index & 1)
                out_ref[pl.ds(start, GX, stride=96), :] = tile


def row_kernel(in_ref, table_ref, out_ref):
    for comp in range(3):
        parts = [
            jnp.concatenate(
                [in_ref[pl.ds((comp * 2 + imag) * 2 + half, ROWS, stride=12), :] for half in range(2)],
                axis=1,
            )
            for imag in range(2)
        ]
        high, low = halves(jnp.concatenate(parts, axis=0))
        value = table_times(table_ref[...], high, low)
        out_ref[comp, 0, 0] = value[:ROWS]
        out_ref[comp, 1, 0] = value[ROWS:]


def exchange(value):
    chunks = value.reshape(GX * GY, 1, -1)
    groups = [[device * 2 + plane for device in ORDER] for plane in range(2)]
    moved = lax.all_to_all(chunks, PLANE, 0, 0, axis_index_groups=groups, tiled=True)
    return moved.reshape(-1, LANES)


def local(toroidal, poloidal):
    vmem = pl.BlockSpec(memory_space=pltpu.VMEM)
    parts = jnp.concatenate([toroidal, poloidal], axis=0)
    packed = parts.reshape(4, ROWS, 2, LANES).transpose(1, 0, 2, 3)
    spread = exchange(packed)
    lines = pl.pallas_call(
        plane_kernel,
        out_shape=jax.ShapeDtypeStruct((ROWS * 12, LANES), jnp.float32),
        in_specs=[vmem] * 6,
        out_specs=vmem,
        scratch_shapes=[pltpu.VMEM((2, 256, 3 * LANES), jnp.bfloat16)] * 2,
        compiler_params=pltpu.CompilerParams(vmem_limit_bytes=32 * 2**20),
    )(spread, outer_tables(), lane_table(), twist_table(), turn_table(), wave_table())
    gathered = exchange(lines)
    return pl.pallas_call(
        row_kernel,
        out_shape=jax.ShapeDtypeStruct((3, 2, 1, ROWS, COLS), jnp.float32),
        in_specs=[vmem, vmem],
        out_specs=vmem,
        compiler_params=pltpu.CompilerParams(vmem_limit_bytes=32 * 2**20),
    )(gathered, row_table())


def solution(mesh):
    in_specs = (P(None, "gz", "gx", "gy"), P(None, "gz", "gx", "gy"))
    out_specs = P(None, None, "gz", "gx", "gy")
    return jax.shard_map(local, mesh=mesh, in_specs=in_specs, out_specs=out_specs, check_vma=False)
```

```python
import math

import jax
import jax.numpy as jnp
import ml_dtypes
import numpy as np
from jax import lax
from jax.experimental import pallas as pl
from jax.experimental.pallas import tpu as pltpu
from jax.sharding import PartitionSpec as P

N = 2048
KZ_FIRST = 128
K0 = 512
GX = 16
GY = 8
ROWS = N // GX
COLS = N // GY
LANES = 128
PLANE = ("gx", "gy", "gz")
GX_ORDER = [11, 7, 15, 6, 13, 5, 9, 4, 10, 3, 12, 2, 8, 1, 14, 0]
GY_ORDER = [7, 5, 3, 6, 1, 4, 2, 0]
ORDER = [gx * GY + gy for gx in GX_ORDER for gy in GY_ORDER]


def reversed_bits(value, nbits):
    return sum(((value >> place) & 1) << (nbits - 1 - place) for place in range(nbits))


def split_table(values, axis):
    high = values.astype(ml_dtypes.bfloat16)
    low = (values - high.astype(np.float64)).astype(ml_dtypes.bfloat16)
    return np.concatenate([high, low], axis)


def outer_tables():
    y0 = np.arange(8)[:, None, None]
    residue = np.array([reversed_bits(d, 4) for d in GX_ORDER])[None, :, None]
    high = (np.array(ORDER) // GY)[None, None, :]
    block = (np.array(ORDER) % GY)[None, None, :]
    tables = []
    for half in range(2):
        phase = (high * residue + (2 * block + half) * y0) % 16
        angle = (2.0 * math.pi / 16) * phase.reshape(128, 128)
        cos, sin = np.cos(angle), np.sin(angle)
        tables.append(split_table(np.block([[cos, -sin], [sin, cos]]), 1))
    return np.stack(tables)


def lane_table():
    lane = np.arange(LANES)
    y1 = 8 * (lane & 15) + (lane >> 4)
    angle = (2.0 * math.pi / LANES) * (lane[:, None] * y1[None, :] % LANES)
    cos, sin = np.cos(angle), np.sin(angle)
    return split_table(np.block([[cos, sin], [-sin, cos]]), 0)


def twist_table():
    angle = (2.0 * math.pi / N) * (-127 * np.arange(16)[:, None] * np.arange(LANES)[None, :] % N)
    return np.stack([np.cos(angle), np.sin(angle)]).astype(np.float32)


def row_table():
    index = np.arange(ROWS)
    angle = (2.0 * math.pi / ROWS) * (index[:, None] * index[None, :] % ROWS)
    cos, sin = np.cos(angle), np.sin(angle)
    return split_table(np.block([[cos, -sin], [sin, cos]]), 1)


def turn_table():
    residue = np.array([reversed_bits(d, 4) for d in GX_ORDER], np.float32) / N
    return np.broadcast_to(residue[:, None], (GX, LANES)).copy()


def wave_table():
    sender = np.array(ORDER)
    base_x = (sender // GY + GX // 2) % GX * ROWS - N // 2
    base_y = (sender % GY + GY // 2) % GY * COLS - N // 2
    rows = np.stack([base_x, base_y]).astype(np.float32)
    return np.broadcast_to(rows[:, :, None], (2, ROWS, LANES)).copy()


def halves(value):
    high = value.astype(jnp.bfloat16)
    return high, (value - high.astype(jnp.float32)).astype(jnp.bfloat16)


def dot(left, right):
    return jnp.dot(left, right, preferred_element_type=jnp.float32)


def table_times(table, high, low):
    wide = jnp.concatenate([table, table[:, : table.shape[1] // 2]], axis=1)
    return dot(wide, jnp.concatenate([high, high, low], axis=0))


def place_in(order, device):
    return sum(jnp.where(device == entry, place, 0) for place, entry in enumerate(order))


def plane_kernel(
    in_ref, outer_ref, lane_ref, twist_ref, turn_ref, wave_ref, out_ref, high_ref, low_ref
):
    low_x = place_in(GX_ORDER, lax.axis_index("gx")) * GY + place_in(GY_ORDER, lax.axis_index("gy"))
    wave_z = (KZ_FIRST + lax.axis_index("gz")).astype(jnp.float32)
    lane = lax.broadcasted_iota(jnp.int32, (ROWS, LANES), 1).astype(jnp.float32)
    wave_x = wave_ref[0] + low_x.astype(jnp.float32)
    for half in range(2):
        wave_y = wave_ref[1] + (lane + half * LANES)
        horiz = wave_x * wave_x + wave_y * wave_y
        square = horiz + wave_z * wave_z
        pol_gain = (4.0 / N / (K0 * K0)) * jnp.exp(1.0 - square * (1.0 / (K0 * K0)))
        tor_gain = pol_gain * jnp.sqrt(square)
        parts = [in_ref[pl.ds(part * 2 + half, ROWS, stride=8), :] for part in range(4)]
        tor_re, tor_im = parts[0] * tor_gain, parts[1] * tor_gain
        pol_re, pol_im = parts[2] * pol_gain, parts[3] * pol_gain
        cross_x, cross_y = wave_x * wave_z, wave_y * wave_z
        spectrum = [
            (-wave_y * tor_im - cross_x * pol_re, wave_y * tor_re - cross_x * pol_im),
            (wave_x * tor_im - cross_y * pol_re, -wave_x * tor_re - cross_y * pol_im),
            (horiz * pol_re, horiz * pol_im),
        ]
        for comp in range(3):
            for imag in range(2):
                high, low = halves(spectrum[comp][imag])
                at = half, pl.ds(imag * ROWS, ROWS), pl.ds(comp * LANES, LANES)
                high_ref[at] = high
                low_ref[at] = low
    turns = low_x.astype(jnp.float32) * turn_ref[...]
    angle = (turns - jnp.floor(turns)) * (2.0 * math.pi)
    turn_re, turn_im = jnp.cos(angle)[None], jnp.sin(angle)[None]
    beta_re, beta_im = twist_ref[0][:, None, :], twist_ref[1][:, None, :]
    twist_re = (beta_re * turn_re - beta_im * turn_im).reshape(256, LANES)
    twist_im = (beta_re * turn_im + beta_im * turn_re).reshape(256, LANES)
    table = lane_ref[...]
    lane_wide = jnp.concatenate([table[:256], table[:256], table[256:]], axis=0)
    lane_bit = lax.broadcasted_iota(jnp.int32, (GX, LANES), 1)
    even, odd = [table_times(outer_ref[h], high_ref[h], low_ref[h]) for h in range(2)]
    for comp in range(3):
        cols = slice(comp * LANES, (comp + 1) * LANES)
        total, differ = even[:, cols] + odd[:, cols], even[:, cols] - odd[:, cols]
        real = jnp.concatenate([total[:ROWS], differ[:ROWS]], axis=0)
        imag = jnp.concatenate([total[ROWS:], differ[ROWS:]], axis=0)
        turned = jnp.concatenate(
            [real * twist_re - imag * twist_im, real * twist_im + imag * twist_re], axis=1
        )
        high, low = halves(turned)
        value = dot(jnp.concatenate([high, low, high], axis=1), lane_wide)
        for imag in range(2):
            tiles = [
                value[y0 * GX : (y0 + 1) * GX, imag * LANES : (imag + 1) * LANES] for y0 in range(16)
            ]
            for place in range(4):
                step = 1 << place
                upper = (lane_bit & step) != 0
                tiles = [jnp.where(upper, tiles[(t + step) % 16], tiles[t]) for t in range(16)]
            for index in range(16):
                tile = tiles[-index % 16]
                if index:
                    source = (lane_bit & 112) + ((lane_bit + index) & 15)
                    tile = jnp.take_along_axis(tile, source, axis=1, mode="promise_in_bounds")
                start = GY_ORDER.index(index >> 1) * 12 + (comp * 2 + imag) * 2 + (index & 1)
                out_ref[pl.ds(start, GX, stride=96), :] = tile


def row_kernel(in_ref, table_ref, out_ref, value_ref, sems):
    copies = []
    for comp in range(3):
        parts = [
            jnp.concatenate(
                [in_ref[pl.ds((comp * 2 + imag) * 2 + half, ROWS, stride=12), :] for half in range(2)],
                axis=1,
            )
            for imag in range(2)
        ]
        high, low = halves(jnp.concatenate(parts, axis=0))
        value = table_times(table_ref[...], high, low)
        value_ref[comp, 0] = value[:ROWS]
        value_ref[comp, 1] = value[ROWS:]
        copies.append(pltpu.make_async_copy(value_ref.at[comp], out_ref.at[comp, :, 0], sems.at[comp]))
        copies[-1].start()
    for copy in copies:
        copy.wait()


def exchange(value):
    chunks = value.reshape(GX * GY, 1, -1)
    groups = [[device * 2 + plane for device in ORDER] for plane in range(2)]
    moved = lax.all_to_all(chunks, PLANE, 0, 0, axis_index_groups=groups, tiled=True)
    return moved.reshape(-1, LANES)


def local(toroidal, poloidal):
    vmem = pl.BlockSpec(memory_space=pltpu.VMEM)
    parts = jnp.concatenate([toroidal, poloidal], axis=0)
    tiles = parts.reshape(4, ROWS // 8, 8, 2, LANES).transpose(0, 1, 3, 2, 4)
    packed = tiles.transpose(1, 3, 0, 2, 4)
    spread = exchange(packed)
    lines = pl.pallas_call(
        plane_kernel,
        out_shape=jax.ShapeDtypeStruct((ROWS * 12, LANES), jnp.float32),
        in_specs=[vmem] * 6,
        out_specs=vmem,
        scratch_shapes=[pltpu.VMEM((2, 256, 3 * LANES), jnp.bfloat16)] * 2,
        compiler_params=pltpu.CompilerParams(vmem_limit_bytes=32 * 2**20),
    )(spread, outer_tables(), lane_table(), twist_table(), turn_table(), wave_table())
    gathered = exchange(lines)
    return pl.pallas_call(
        row_kernel,
        out_shape=jax.ShapeDtypeStruct((3, 2, 1, ROWS, COLS), jnp.float32),
        in_specs=[vmem, vmem],
        out_specs=pl.BlockSpec(memory_space=pl.ANY),
        scratch_shapes=[
            pltpu.VMEM((3, 2, ROWS, COLS), jnp.float32),
            pltpu.SemaphoreType.DMA((3,)),
        ],
        compiler_params=pltpu.CompilerParams(vmem_limit_bytes=32 * 2**20),
    )(gathered, row_table())


def solution(mesh):
    in_specs = (P(None, "gz", "gx", "gy"), P(None, "gz", "gx", "gy"))
    out_specs = P(None, None, "gz", "gx", "gy")
    return jax.shard_map(local, mesh=mesh, in_specs=in_specs, out_specs=out_specs, check_vma=False)
```

```python
import math

import jax
import jax.numpy as jnp
import ml_dtypes
import numpy as np
from jax import lax
from jax.experimental import pallas as pl
from jax.experimental.pallas import tpu as pltpu
from jax.sharding import PartitionSpec as P

N = 2048
KZ_FIRST = 128
K0 = 512
GX = 16
GY = 8
ROWS = N // GX
COLS = N // GY
LANES = 128
PLANE = ("gx", "gy", "gz")
GX_ORDER = [8, 1, 12, 5, 15, 7, 14, 4, 13, 2, 10, 3, 9, 0, 11, 6]
GY_ORDER = [7, 5, 3, 6, 1, 4, 2, 0]
ORDER = [gx * GY + gy for gx in GX_ORDER for gy in GY_ORDER]


def reversed_bits(value, nbits):
    return sum(((value >> place) & 1) << (nbits - 1 - place) for place in range(nbits))


def split_table(values, axis):
    high = values.astype(ml_dtypes.bfloat16)
    low = (values - high.astype(np.float64)).astype(ml_dtypes.bfloat16)
    return np.concatenate([high, low], axis)


def outer_tables():
    y0 = np.arange(8)[:, None, None]
    residue = np.array([reversed_bits(d, 4) for d in GX_ORDER])[None, :, None]
    high = (np.array(ORDER) // GY)[None, None, :]
    block = (np.array(ORDER) % GY)[None, None, :]
    tables = []
    for half in range(2):
        phase = (high * residue + (2 * block + half) * y0) % 16
        angle = (2.0 * math.pi / 16) * phase.reshape(128, 128)
        cos, sin = np.cos(angle), np.sin(angle)
        tables.append(split_table(np.block([[cos, -sin], [sin, cos]]), 1))
    return np.stack(tables)


def lane_table():
    lane = np.arange(LANES)
    y1 = 8 * (lane & 15) + (lane >> 4)
    angle = (2.0 * math.pi / LANES) * (lane[:, None] * y1[None, :] % LANES)
    cos, sin = np.cos(angle), np.sin(angle)
    return split_table(np.block([[cos, sin], [-sin, cos]]), 0)


def twist_table():
    angle = (2.0 * math.pi / N) * (-127 * np.arange(16)[:, None] * np.arange(LANES)[None, :] % N)
    return np.stack([np.cos(angle), np.sin(angle)]).astype(np.float32)


def row_table():
    index = np.arange(ROWS)
    angle = (2.0 * math.pi / ROWS) * (index[:, None] * index[None, :] % ROWS)
    cos, sin = np.cos(angle), np.sin(angle)
    return split_table(np.block([[cos, -sin], [sin, cos]]), 1)


def turn_table():
    residue = np.array([reversed_bits(d, 4) for d in GX_ORDER], np.float32) / N
    return np.broadcast_to(residue[:, None], (GX, LANES)).copy()


def wave_table():
    sender = np.array(ORDER)
    base_x = (sender // GY + GX // 2) % GX * ROWS - N // 2
    base_y = (sender % GY + GY // 2) % GY * COLS - N // 2
    rows = np.stack([base_x, base_y]).astype(np.float32)
    return np.broadcast_to(rows[:, :, None], (2, ROWS, LANES)).copy()


def halves(value):
    high = value.astype(jnp.bfloat16)
    return high, (value - high.astype(jnp.float32)).astype(jnp.bfloat16)


def dot(left, right):
    return jnp.dot(left, right, preferred_element_type=jnp.float32)


def table_times(table, high, low):
    wide = jnp.concatenate([table, table[:, : table.shape[1] // 2]], axis=1)
    return dot(wide, jnp.concatenate([high, high, low], axis=0))


def place_in(order, device):
    return sum(jnp.where(device == entry, place, 0) for place, entry in enumerate(order))


def plane_kernel(
    in_ref, outer_ref, lane_ref, twist_ref, turn_ref, wave_ref, out_ref, high_ref, low_ref
):
    low_x = place_in(GX_ORDER, lax.axis_index("gx")) * GY + place_in(GY_ORDER, lax.axis_index("gy"))
    wave_z = (KZ_FIRST + lax.axis_index("gz")).astype(jnp.float32)
    lane = lax.broadcasted_iota(jnp.int32, (ROWS, LANES), 1).astype(jnp.float32)
    wave_x = wave_ref[0] + low_x.astype(jnp.float32)
    for half in range(2):
        wave_y = wave_ref[1] + (lane + half * LANES)
        horiz = wave_x * wave_x + wave_y * wave_y
        square = horiz + wave_z * wave_z
        pol_gain = (4.0 / N / (K0 * K0)) * jnp.exp(1.0 - square * (1.0 / (K0 * K0)))
        tor_gain = pol_gain * jnp.sqrt(square)
        parts = [in_ref[pl.ds(part * 2 + half, ROWS, stride=8), :] for part in range(4)]
        tor_re, tor_im = parts[0] * tor_gain, parts[1] * tor_gain
        pol_re, pol_im = parts[2] * pol_gain, parts[3] * pol_gain
        cross_x, cross_y = wave_x * wave_z, wave_y * wave_z
        spectrum = [
            (-wave_y * tor_im - cross_x * pol_re, wave_y * tor_re - cross_x * pol_im),
            (wave_x * tor_im - cross_y * pol_re, -wave_x * tor_re - cross_y * pol_im),
            (horiz * pol_re, horiz * pol_im),
        ]
        for comp in range(3):
            for imag in range(2):
                high, low = halves(spectrum[comp][imag])
                at = half, pl.ds(imag * ROWS, ROWS), pl.ds(comp * LANES, LANES)
                high_ref[at] = high
                low_ref[at] = low
    turns = low_x.astype(jnp.float32) * turn_ref[...]
    angle = (turns - jnp.floor(turns)) * (2.0 * math.pi)
    turn_re, turn_im = jnp.cos(angle)[None], jnp.sin(angle)[None]
    beta_re, beta_im = twist_ref[0][:, None, :], twist_ref[1][:, None, :]
    twist_re = (beta_re * turn_re - beta_im * turn_im).reshape(256, LANES)
    twist_im = (beta_re * turn_im + beta_im * turn_re).reshape(256, LANES)
    table = lane_ref[...]
    lane_wide = jnp.concatenate([table[:256], table[:256], table[256:]], axis=0)
    lane_bit = lax.broadcasted_iota(jnp.int32, (GX, LANES), 1)
    even, odd = [table_times(outer_ref[h], high_ref[h], low_ref[h]) for h in range(2)]
    for comp in range(3):
        cols = slice(comp * LANES, (comp + 1) * LANES)
        total, differ = even[:, cols] + odd[:, cols], even[:, cols] - odd[:, cols]
        real = jnp.concatenate([total[:ROWS], differ[:ROWS]], axis=0)
        imag = jnp.concatenate([total[ROWS:], differ[ROWS:]], axis=0)
        turned = jnp.concatenate(
            [real * twist_re - imag * twist_im, real * twist_im + imag * twist_re], axis=1
        )
        high, low = halves(turned)
        value = dot(jnp.concatenate([high, low, high], axis=1), lane_wide)
        for imag in range(2):
            tiles = [
                value[y0 * GX : (y0 + 1) * GX, imag * LANES : (imag + 1) * LANES] for y0 in range(16)
            ]
            for place in range(4):
                step = 1 << place
                upper = (lane_bit & step) != 0
                tiles = [jnp.where(upper, tiles[(t + step) % 16], tiles[t]) for t in range(16)]
            for index in range(16):
                tile = tiles[-index % 16]
                if index:
                    source = (lane_bit & 112) + ((lane_bit + index) & 15)
                    tile = jnp.take_along_axis(tile, source, axis=1, mode="promise_in_bounds")
                start = GY_ORDER.index(index >> 1) * 12 + (comp * 2 + imag) * 2 + (index & 1)
                out_ref[pl.ds(start, GX, stride=96), :] = tile


def row_kernel(in_ref, table_ref, out_ref, value_ref, sems):
    copies = []
    for comp in range(3):
        parts = [
            jnp.concatenate(
                [in_ref[pl.ds((comp * 2 + imag) * 2 + half, ROWS, stride=12), :] for half in range(2)],
                axis=1,
            )
            for imag in range(2)
        ]
        high, low = halves(jnp.concatenate(parts, axis=0))
        value = table_times(table_ref[...], high, low)
        value_ref[comp, 0] = value[:ROWS]
        value_ref[comp, 1] = value[ROWS:]
        copies.append(pltpu.make_async_copy(value_ref.at[comp], out_ref.at[comp, :, 0], sems.at[comp]))
        copies[-1].start()
    for copy in copies:
        copy.wait()


def exchange(value):
    chunks = value.reshape(GX * GY, 1, -1)
    groups = [[device * 2 + plane for device in ORDER] for plane in range(2)]
    moved = lax.all_to_all(chunks, PLANE, 0, 0, axis_index_groups=groups, tiled=True)
    return moved.reshape(-1, LANES)


def local(toroidal, poloidal):
    vmem = pl.BlockSpec(memory_space=pltpu.VMEM)
    parts = jnp.concatenate([toroidal, poloidal], axis=0)
    tiles = parts.reshape(4, ROWS // 8, 8, 2, LANES).transpose(0, 1, 3, 2, 4)
    packed = tiles.transpose(1, 3, 0, 2, 4)
    spread = exchange(packed)
    lines = pl.pallas_call(
        plane_kernel,
        out_shape=jax.ShapeDtypeStruct((ROWS * 12, LANES), jnp.float32),
        in_specs=[vmem] * 6,
        out_specs=vmem,
        scratch_shapes=[pltpu.VMEM((2, 256, 3 * LANES), jnp.bfloat16)] * 2,
        compiler_params=pltpu.CompilerParams(vmem_limit_bytes=32 * 2**20),
    )(spread, outer_tables(), lane_table(), twist_table(), turn_table(), wave_table())
    gathered = exchange(lines)
    return pl.pallas_call(
        row_kernel,
        out_shape=jax.ShapeDtypeStruct((3, 2, 1, ROWS, COLS), jnp.float32),
        in_specs=[vmem, vmem],
        out_specs=pl.BlockSpec(memory_space=pl.ANY),
        scratch_shapes=[
            pltpu.VMEM((3, 2, ROWS, COLS), jnp.float32),
            pltpu.SemaphoreType.DMA((3,)),
        ],
        compiler_params=pltpu.CompilerParams(vmem_limit_bytes=32 * 2**20),
    )(gathered, row_table())


def solution(mesh):
    in_specs = (P(None, "gz", "gx", "gy"), P(None, "gz", "gx", "gy"))
    out_specs = P(None, None, "gz", "gx", "gy")
    return jax.shard_map(local, mesh=mesh, in_specs=in_specs, out_specs=out_specs, check_vma=False)
```

```python
import math

import jax
import jax.numpy as jnp
import ml_dtypes
import numpy as np
from jax import lax
from jax.experimental import pallas as pl
from jax.experimental.pallas import tpu as pltpu
from jax.sharding import PartitionSpec as P

N = 2048
KZ_FIRST = 128
K0 = 512
GX = 16
GY = 8
ROWS = N // GX
COLS = N // GY
LANES = 128
PLANE = ("gx", "gy", "gz")
GX_ORDER = [11, 7, 15, 6, 13, 5, 9, 4, 10, 3, 12, 2, 8, 1, 14, 0]
GY_ORDER = [7, 5, 3, 6, 1, 4, 2, 0]
ORDER = [gx * GY + gy for gx in GX_ORDER for gy in GY_ORDER]


def reversed_bits(value, nbits):
    return sum(((value >> place) & 1) << (nbits - 1 - place) for place in range(nbits))


def split_table(values, axis):
    high = values.astype(ml_dtypes.bfloat16)
    low = (values - high.astype(np.float64)).astype(ml_dtypes.bfloat16)
    return np.concatenate([high, low], axis)


def outer_tables():
    y0 = np.arange(8)[:, None, None]
    residue = np.array([reversed_bits(d, 4) for d in GX_ORDER])[None, :, None]
    high = (np.array(ORDER) // GY)[None, None, :]
    block = (np.array(ORDER) % GY)[None, None, :]
    tables = []
    for half in range(2):
        phase = (high * residue + (2 * block + half) * y0) % 16
        angle = (2.0 * math.pi / 16) * phase.reshape(128, 128)
        cos, sin = np.cos(angle), np.sin(angle)
        tables.append(split_table(np.block([[cos, -sin], [sin, cos]]), 1))
    return np.stack(tables)


def lane_table():
    lane = np.arange(LANES)
    y1 = 8 * (lane & 15) + (lane >> 4)
    angle = (2.0 * math.pi / LANES) * (lane[:, None] * y1[None, :] % LANES)
    cos, sin = np.cos(angle), np.sin(angle)
    return split_table(np.block([[cos, sin], [-sin, cos]]), 0)


def twist_table():
    angle = (2.0 * math.pi / N) * (-127 * np.arange(16)[:, None] * np.arange(LANES)[None, :] % N)
    return np.stack([np.cos(angle), np.sin(angle)]).astype(np.float32)


def row_table():
    index = np.arange(ROWS)
    angle = (2.0 * math.pi / ROWS) * (index[:, None] * index[None, :] % ROWS)
    cos, sin = np.cos(angle), np.sin(angle)
    return split_table(np.block([[cos, -sin], [sin, cos]]), 1)


def turn_table():
    residue = np.array([reversed_bits(d, 4) for d in GX_ORDER], np.float32) / N
    return np.broadcast_to(residue[:, None], (GX, LANES)).copy()


def wave_table():
    sender = np.array(ORDER)
    base_x = (sender // GY + GX // 2) % GX * ROWS - N // 2
    base_y = (sender % GY + GY // 2) % GY * COLS - N // 2
    rows = np.stack([base_x, base_y]).astype(np.float32)
    return np.broadcast_to(rows[:, :, None], (2, ROWS, LANES)).copy()


def halves(value):
    high = value.astype(jnp.bfloat16)
    return high, (value - high.astype(jnp.float32)).astype(jnp.bfloat16)


def dot(left, right):
    return jnp.dot(left, right, preferred_element_type=jnp.float32)


def table_times(table, high, low):
    wide = jnp.concatenate([table, table[:, : table.shape[1] // 2]], axis=1)
    return dot(wide, jnp.concatenate([high, high, low], axis=0))


def place_in(order, device):
    return sum(jnp.where(device == entry, place, 0) for place, entry in enumerate(order))


def plane_kernel(
    in_ref, outer_ref, lane_ref, twist_ref, turn_ref, wave_ref, out_ref, high_ref, low_ref
):
    low_x = place_in(GX_ORDER, lax.axis_index("gx")) * GY + place_in(GY_ORDER, lax.axis_index("gy"))
    wave_z = (KZ_FIRST + lax.axis_index("gz")).astype(jnp.float32)
    lane = lax.broadcasted_iota(jnp.int32, (ROWS, LANES), 1).astype(jnp.float32)
    wave_x = wave_ref[0] + low_x.astype(jnp.float32)
    for half in range(2):
        wave_y = wave_ref[1] + (lane + half * LANES)
        horiz = wave_x * wave_x + wave_y * wave_y
        square = horiz + wave_z * wave_z
        pol_gain = (4.0 / N / (K0 * K0)) * jnp.exp(1.0 - square * (1.0 / (K0 * K0)))
        tor_gain = pol_gain * jnp.sqrt(square)
        parts = [in_ref[pl.ds(part * 2 + half, ROWS, stride=8), :] for part in range(4)]
        tor_re, tor_im = parts[0] * tor_gain, parts[1] * tor_gain
        pol_re, pol_im = parts[2] * pol_gain, parts[3] * pol_gain
        cross_x, cross_y = wave_x * wave_z, wave_y * wave_z
        spectrum = [
            (-wave_y * tor_im - cross_x * pol_re, wave_y * tor_re - cross_x * pol_im),
            (wave_x * tor_im - cross_y * pol_re, -wave_x * tor_re - cross_y * pol_im),
            (horiz * pol_re, horiz * pol_im),
        ]
        for comp in range(3):
            for imag in range(2):
                high, low = halves(spectrum[comp][imag])
                at = half, pl.ds(imag * ROWS, ROWS), pl.ds(comp * LANES, LANES)
                high_ref[at] = high
                low_ref[at] = low
    turns = low_x.astype(jnp.float32) * turn_ref[...]
    angle = (turns - jnp.floor(turns)) * (2.0 * math.pi)
    turn_re, turn_im = jnp.cos(angle)[None], jnp.sin(angle)[None]
    beta_re, beta_im = twist_ref[0][:, None, :], twist_ref[1][:, None, :]
    twist_re = (beta_re * turn_re - beta_im * turn_im).reshape(256, LANES)
    twist_im = (beta_re * turn_im + beta_im * turn_re).reshape(256, LANES)
    table = lane_ref[...]
    lane_wide = jnp.concatenate([table[:256], table[:256], table[256:]], axis=0)
    lane_bit = lax.broadcasted_iota(jnp.int32, (GX, LANES), 1)
    even, odd = [table_times(outer_ref[h], high_ref[h], low_ref[h]) for h in range(2)]
    for comp in range(3):
        cols = slice(comp * LANES, (comp + 1) * LANES)
        total, differ = even[:, cols] + odd[:, cols], even[:, cols] - odd[:, cols]
        real = jnp.concatenate([total[:ROWS], differ[:ROWS]], axis=0)
        imag = jnp.concatenate([total[ROWS:], differ[ROWS:]], axis=0)
        turned = jnp.concatenate(
            [real * twist_re - imag * twist_im, real * twist_im + imag * twist_re], axis=1
        )
        high, low = halves(turned)
        value = dot(jnp.concatenate([high, low, high], axis=1), lane_wide)
        for imag in range(2):
            tiles = [
                value[y0 * GX : (y0 + 1) * GX, imag * LANES : (imag + 1) * LANES] for y0 in range(16)
            ]
            for place in range(4):
                step = 1 << place
                upper = (lane_bit & step) != 0
                tiles = [jnp.where(upper, tiles[(t + step) % 16], tiles[t]) for t in range(16)]
            for index in range(16):
                tile = tiles[-index % 16]
                if index:
                    source = (lane_bit & 112) + ((lane_bit + index) & 15)
                    tile = jnp.take_along_axis(tile, source, axis=1, mode="promise_in_bounds")
                start = GY_ORDER.index(index >> 1) * 12 + (comp * 2 + imag) * 2 + (index & 1)
                out_ref[pl.ds(start, GX, stride=96), :] = tile


def row_kernel(in_ref, table_ref, out_ref, value_ref, sems):
    copies = []
    for comp in range(3):
        parts = [
            jnp.concatenate(
                [in_ref[pl.ds((comp * 2 + imag) * 2 + half, ROWS, stride=12), :] for half in range(2)],
                axis=1,
            )
            for imag in range(2)
        ]
        high, low = halves(jnp.concatenate(parts, axis=0))
        value = table_times(table_ref[...], high, low)
        for imag in range(2):
            value_ref[comp, imag] = value[imag * ROWS : (imag + 1) * ROWS]
            source, target = value_ref.at[comp, imag], out_ref.at[comp, imag, 0]
            copies.append(pltpu.make_async_copy(source, target, sems.at[comp * 2 + imag]))
            copies[-1].start()
    for copy in copies:
        copy.wait()


def exchange(value):
    chunks = value.reshape(GX * GY, 1, -1)
    groups = [[device * 2 + plane for device in ORDER] for plane in range(2)]
    moved = lax.all_to_all(chunks, PLANE, 0, 0, axis_index_groups=groups, tiled=True)
    return moved.reshape(-1, LANES)


def local(toroidal, poloidal):
    vmem = pl.BlockSpec(memory_space=pltpu.VMEM)
    parts = jnp.concatenate([toroidal, poloidal], axis=0)
    tiles = parts.reshape(4, ROWS // 8, 8, 2, LANES).transpose(0, 1, 3, 2, 4)
    packed = tiles.transpose(1, 3, 0, 2, 4)
    spread = exchange(packed)
    lines = pl.pallas_call(
        plane_kernel,
        out_shape=jax.ShapeDtypeStruct((ROWS * 12, LANES), jnp.float32),
        in_specs=[vmem] * 6,
        out_specs=vmem,
        scratch_shapes=[pltpu.VMEM((2, 256, 3 * LANES), jnp.bfloat16)] * 2,
        compiler_params=pltpu.CompilerParams(vmem_limit_bytes=32 * 2**20),
    )(spread, outer_tables(), lane_table(), twist_table(), turn_table(), wave_table())
    gathered = exchange(lines)
    return pl.pallas_call(
        row_kernel,
        out_shape=jax.ShapeDtypeStruct((3, 2, 1, ROWS, COLS), jnp.float32),
        in_specs=[vmem, vmem],
        out_specs=pl.BlockSpec(memory_space=pl.ANY),
        scratch_shapes=[
            pltpu.VMEM((3, 2, ROWS, COLS), jnp.float32),
            pltpu.SemaphoreType.DMA((6,)),
        ],
        compiler_params=pltpu.CompilerParams(vmem_limit_bytes=32 * 2**20),
    )(gathered, row_table())


def solution(mesh):
    in_specs = (P(None, "gz", "gx", "gy"), P(None, "gz", "gx", "gy"))
    out_specs = P(None, None, "gz", "gx", "gy")
    return jax.shard_map(local, mesh=mesh, in_specs=in_specs, out_specs=out_specs, check_vma=False)
```
